32 devices in a mesh: space: 8 (over y, x, core), vel: 4 (over z).
Axes of the slice: x: 2, y: 2, z: 4, core: 2. Of those that a mesh axis runs over, the one named last changes fastest.
Arguments:
- distribution: float32 [4096, 8192], P('vel', 'space'), may hold values from -48 to 48
- kernel: bfloat16 [4096, 4096], P('vel'), may hold values from -0.046875 to 0.046875
- frequency: float32 [4096], P('vel'), may hold values from 0.05 to 0.5
- accommodation: float32 [8], replicated, may hold values from 0.2 to 0.95
- wall_class: int32 [2, 256], P(None, 'space'), may hold values from 0 to 7
Outputs:
- updated: float32 [4096, 8192], P('vel', 'space')
The draws below stay inside these ranges and needn't reach their ends.
All inputs are finite; a program needn't handle non-finite values.
Results may differ from the reference program's by a relative error of at most 0.0018.
Values may be sent and summed in bfloat16 or wider, within the bound.
A program may use at most 128 MiB of HBM per device.

```python
import math
import jax
import jax.numpy as jnp

NV1 = 16
V = 4096
NY = 32
NX = 256
NCLASS = 8


def draw_distribution(key, part):
    key_rows, key_cols, key_noise = jax.random.split(key, 3)
    row_scale = jnp.exp(jax.random.uniform(key_rows, (V, 1), jnp.float32, math.log(0.3), math.log(3.0)))
    col_scale = jnp.exp(jax.random.uniform(key_cols, (1, NX * NY), jnp.float32, math.log(0.4), math.log(4.0)))
    noise = jax.random.truncated_normal(key_noise, -4.0, 4.0, (V, NX * NY), jnp.float32)
    return row_scale * noise * col_scale


def set_ends(drawn, own_key, low, largest):
    shape = drawn.shape
    spot = [jax.random.randint(jax.random.fold_in(own_key, axis), (), 0, shape[axis]) for axis in range(len(shape))]
    drawn = drawn.at[tuple(spot)].set(low)
    longest = shape.index(max(shape))
    spot[longest] = (spot[longest] + 1) % shape[longest]
    return drawn.at[tuple(spot)].set(largest)


def shard_levels(own_key, dims, cuts, low, high):
    loudness, own = 1.0, jax.random.fold_in(own_key, 6)
    for axis_at, blocks in cuts:
        draws = jnp.exp(jax.random.uniform(jax.random.fold_in(own, axis_at), (blocks,), jnp.float32, low / len(cuts), high / len(cuts)))
        loudness = loudness * jnp.repeat(draws, dims[axis_at] // blocks).reshape([-1 if axis == axis_at else 1 for axis in range(len(dims))])
    return loudness


def gaussian(stream_key, dims, scale, most, cuts=(), held_as=jnp.bfloat16):
    drawn = scale * jax.random.normal(stream_key, dims, jnp.float32)
    if cuts:
        drawn = drawn * shard_levels(stream_key, dims, cuts, -0.22, 0.18)
    return jnp.clip(drawn, -most, most).astype(held_as)


def setup_inputs(seed: int = 0) -> dict:
    key_list = jax.random.split(jax.random.key(seed), 6)
    return {
        "distribution": draw_distribution(jax.random.fold_in(key_list[5], 71), 0),
        "kernel": gaussian(key_list[1], (V, V), (4 * V) ** -0.5, 0.046875, ((0, 4),)),
        "frequency": jnp.clip(jnp.exp(math.log(0.5) - 2.3025851 * jax.random.uniform(key_list[2], (V,), jnp.float32) ** shard_levels(key_list[2], (V,), ((0, 4),), -0.2, 0.2)), 0.05, 0.5),
        "accommodation": jnp.clip(jax.random.uniform(key_list[3], (NCLASS,), jnp.float32, 0.2, 0.95), 0.2, 0.95),
        "wall_class": set_ends(jax.random.randint(key_list[4], (2, NX), 0, NCLASS), jax.random.fold_in(key_list[4], 1), 0, NCLASS - 1).astype(jnp.int32),
    }


courant_x = 0.05
courant_y = 0.15


def velocity_parts(vel_index):
    spacing = 9.6 / NV1
    middle = (NV1 - 1) / 2.0
    index_y = vel_index // (NV1 * NV1)
    index_x = (vel_index // NV1) % NV1
    index_z = vel_index % NV1
    vel_x = (index_x.astype(jnp.float32) - middle) * spacing
    vel_y = (index_y.astype(jnp.float32) - middle) * spacing
    vel_z = (index_z.astype(jnp.float32) - middle) * spacing
    return vel_x, vel_y, vel_z


def grid_constants():
    spacing = 9.6 / NV1
    middle = (NV1 - 1) / 2.0
    points = (jnp.arange(NV1, dtype=jnp.int32).astype(jnp.float32) - middle) * spacing
    weights = jnp.exp(-0.5 * points * points)
    zsum = jnp.sum(weights)
    outflow = jnp.sum(jnp.where(points > 0, points * weights, 0.0)) / zsum
    return zsum * zsum * zsum, outflow


def reference(distribution, kernel, frequency, accommodation, wall_class):
    vel_x, vel_y, vel_z = velocity_parts(jnp.arange(V, dtype=jnp.int32))
    normal_sum, outflow = grid_constants()
    maxwell = jnp.exp(-0.5 * (vel_x * vel_x + vel_y * vel_y + vel_z * vel_z)) / normal_sum
    field = distribution.reshape(V, NX, NY)
    lowered = distribution.astype(jnp.bfloat16)
    low_field = lowered.reshape(V, NX, NY)
    lower = low_field[:, :, 0].astype(jnp.float32)
    upper = low_field[:, :, NY - 1].astype(jnp.float32)
    down_weight = jnp.where(vel_y < 0, -vel_y, 0.0)
    up_weight = jnp.where(vel_y > 0, vel_y, 0.0)
    sigma_low = jnp.sum(down_weight[:, None] * lower, axis=0) / outflow
    sigma_up = jnp.sum(up_weight[:, None] * upper, axis=0) / outflow
    alpha = accommodation[wall_class]
    mirror_low = lower.reshape(NV1, NV1 * NV1, NX)[::-1].reshape(V, NX)
    mirror_up = upper.reshape(NV1, NV1 * NV1, NX)[::-1].reshape(V, NX)
    inflow_low = alpha[0][None, :] * sigma_low[None, :] * maxwell[:, None] + (1.0 - alpha[0])[None, :] * mirror_low
    inflow_up = alpha[1][None, :] * sigma_up[None, :] * maxwell[:, None] + (1.0 - alpha[1])[None, :] * mirror_up
    left = jnp.roll(field, 1, axis=1)
    right = jnp.roll(field, -1, axis=1)
    below = jnp.concatenate([inflow_low[:, :, None], field[:, :, :-1]], axis=2)
    above = jnp.concatenate([field[:, :, 1:], inflow_up[:, :, None]], axis=2)
    move_x = courant_x * (jnp.maximum(vel_x, 0.0)[:, None, None] * (field - left) + jnp.minimum(vel_x, 0.0)[:, None, None] * (right - field))
    move_y = courant_y * (jnp.maximum(vel_y, 0.0)[:, None, None] * (field - below) + jnp.minimum(vel_y, 0.0)[:, None, None] * (above - field))
    moved = (move_x + move_y).reshape(V, NX * NY)
    gain = jnp.dot(kernel, lowered, preferred_element_type=jnp.float32)
    return distribution - moved - frequency[:, None] * distribution + gain
```

```python
import jax
import jax.numpy as jnp
from jax import lax
from jax.experimental import pallas as pl
from jax.experimental.pallas import tpu as pltpu
from jax.sharding import PartitionSpec as P

NV1 = 16
NY = 32
NCLASS = 8


courant_x = 0.05
courant_y = 0.15


def swapped(value, axis, distance):
    return lax.ppermute(value, axis, [(i, i ^ 1 << distance) for i in range(lax.axis_size(axis))])


def extended(value, sides, width):
    for axis, dim in sides:
        devices, length = (lax.axis_size(axis), value.shape[dim])
        up = [(i, (i + 1) % devices) for i in range(devices)]
        down = [(j, i) for i, j in up]
        last = lax.slice_in_dim(value, length - width, length, axis=dim)
        initial = lax.slice_in_dim(value, 0, width, axis=dim)
        before = lax.ppermute(last, axis, up)
        after = lax.ppermute(initial, axis, down)
        value = jnp.concatenate([before, value, after], axis=dim)
    return value


def velocity_parts(vel_index):
    spacing = 9.6 / NV1
    middle = (NV1 - 1) / 2.0
    index_y = vel_index // (NV1 * NV1)
    index_x = vel_index // NV1 % NV1
    index_z = vel_index % NV1
    vel_x = (index_x.astype(jnp.float32) - middle) * spacing
    vel_y = (index_y.astype(jnp.float32) - middle) * spacing
    vel_z = (index_z.astype(jnp.float32) - middle) * spacing
    return (vel_x, vel_y, vel_z)


def grid_constants():
    spacing = 9.6 / NV1
    middle = (NV1 - 1) / 2.0
    points = (lax.iota(jnp.int32, NV1).astype(jnp.float32) - middle) * spacing
    weights = jnp.exp(-0.5 * points * points)
    zsum = jnp.sum(weights)
    outflow = jnp.sum(jnp.where(points > 0, points * weights, 0.0)) / zsum
    return (zsum * zsum * zsum, outflow)


def per_device(distribution, kernel, frequency, accommodation, wall_class):
    vel_rows, cell_count = distribution.shape
    columns = cell_count // NY
    plane = NV1 * NV1
    rank = lax.axis_index("vel")
    vel_index = rank * vel_rows + lax.iota(jnp.int32, vel_rows)
    vel_x, vel_y, vel_z = velocity_parts(vel_index)
    normal_sum, outflow = grid_constants()
    maxwell = jnp.exp(-0.5 * (vel_x * vel_x + vel_y * vel_y + vel_z * vel_z)) / normal_sum
    lowered = distribution.astype(jnp.bfloat16)
    walls = jnp.stack([lowered[:, 0::NY], lowered[:, NY - 1 :: NY]])
    wide = walls.astype(jnp.float32)
    down_weight = jnp.where(vel_y < 0, -vel_y, 0.0)
    up_weight = jnp.where(vel_y > 0, vel_y, 0.0)
    partial_flux = jnp.stack(
        [
            jnp.sum(down_weight[:, None] * wide[0], axis=0),
            jnp.sum(up_weight[:, None] * wide[1], axis=0),
        ]
    )
    flux = lax.psum(partial_flux, "vel")
    mirrored = walls
    log_rows = vel_rows.bit_length() - 1
    log_devices = lax.axis_size("vel").bit_length() - 1
    log_plane = 2 * (NV1.bit_length() - 1)
    for bit_index in range(max(log_plane - log_rows, 0), log_devices):
        mirrored = swapped(mirrored, "vel", bit_index)
    if vel_rows > plane:
        mirrored = mirrored.reshape(2, vel_rows // plane, plane, columns)[:, ::-1].reshape(
            2, vel_rows, columns
        )
    mirrored = mirrored.astype(jnp.float32)
    sigma = flux / outflow
    class_ids = lax.iota(jnp.int32, NCLASS)
    alpha = jnp.sum(
        jnp.where(
            wall_class[:, :, None] == class_ids[None, None, :], accommodation[None, None, :], 0.0
        ),
        axis=2,
    )
    inflow = (
        alpha[:, None, :] * sigma[:, None, :] * maxwell[None, :, None]
        + (1.0 - alpha)[:, None, :] * mirrored
    )
    padded = extended(distribution.astype(jnp.bfloat16), (("space", 1),), NY).astype(
        distribution.dtype
    )
    left = padded[:, :cell_count]
    right = padded[:, 2 * NY :]
    y_place = lax.iota(jnp.int32, cell_count) % NY
    below = jnp.concatenate([distribution[:, :1], distribution[:, :-1]], axis=1)
    below = jnp.where(y_place[None, :] == 0, jnp.repeat(inflow[0], NY, axis=1), below)
    above = jnp.concatenate([distribution[:, 1:], distribution[:, -1:]], axis=1)
    above = jnp.where(y_place[None, :] == NY - 1, jnp.repeat(inflow[1], NY, axis=1), above)
    move_x = courant_x * (
        jnp.maximum(vel_x, 0.0)[:, None] * (distribution - left)
        + jnp.minimum(vel_x, 0.0)[:, None] * (right - distribution)
    )
    move_y = courant_y * (
        jnp.maximum(vel_y, 0.0)[:, None] * (distribution - below)
        + jnp.minimum(vel_y, 0.0)[:, None] * (above - distribution)
    )
    moved = move_x + move_y
    shard_piece = lax.all_gather(lowered, "vel", axis=0, tiled=True)
    running = jnp.dot(kernel, shard_piece, preferred_element_type=jnp.float32)
    piece_walls = jnp.stack([shard_piece[:, 0::NY], shard_piece[:, NY - 1 :: NY]])
    wall_store = piece_walls
    gain, wall_store = (running, wall_store)
    return distribution - moved - frequency[:, None] * distribution + gain


WIDE = 128
ROWS = 1024
TILE = NV1 * NV1
PARTS = 4
SPACE = 8


def gain_kernel(dist, kern, coef, lanes, out, d32, ks, ke, db, pb, hl,
                lsem, s1, r1, s2, r2, s3, r3, s4, r4, sk, rk, sh, rh):
    chunks = dist.shape[1] // WIDE
    sp, z = lax.axis_index("space"), lax.axis_index("vel")
    half = lax.div(z, 2)
    mid = lax.rem(z, 2) + half == 1
    mate = z + 1 - 2 * lax.rem(z, 2)
    peer = 3 - z
    far = 3 - mate
    by_core = sp + 1 - 2 * lax.rem(sp, 2)
    by_x = sp + 2 - 4 * lax.rem(lax.div(sp, 2), 2)
    by_y = sp + 4 - 8 * lax.div(sp, 4)
    by_xy = by_x + by_y - sp
    right = lax.rem(sp + 1, SPACE)
    left = lax.rem(sp + SPACE - 1, SPACE)

    def remote(src, dst, send, recv, space, vel):
        return pltpu.make_async_remote_copy(
            src_ref=src, dst_ref=dst, send_sem=send, recv_sem=recv,
            device_id={"space": space, "vel": vel}, device_id_type=pl.DeviceIdType.MESH)

    load_d = pltpu.make_async_copy(dist, d32, lsem.at[0])
    load_k = pltpu.make_async_copy(kern, ks, lsem.at[1])
    load_d.start()
    load_k.start()

    barrier = pltpu.get_barrier_semaphore()

    def greet(space, vel):
        pl.semaphore_signal(barrier, inc=1, device_id={"space": space, "vel": vel},
                            device_id_type=pl.DeviceIdType.MESH)

    greet(sp, mate)
    greet(left, z)
    greet(right, z)

    @pl.when(mid)
    def _():
        greet(sp, peer)
        greet(by_core, z)
        greet(by_x, z)
        greet(by_y, z)
        pl.semaphore_wait(barrier, 7)

    @pl.when(jnp.logical_not(mid))
    def _():
        pl.semaphore_wait(barrier, 3)

    def slab(owner):
        return ke.at[pl.ds(pl.multiple_of(owner * (ROWS // SPACE), ROWS // SPACE), ROWS // SPACE)]

    slab_rows = pl.ds(pl.multiple_of(sp * (ROWS // SPACE), ROWS // SPACE), ROWS // SPACE)
    slab_cols = pl.ds(pl.multiple_of((1 - half) * 2 * ROWS, 2 * ROWS), 2 * ROWS)
    kern_out = remote(kern.at[slab_rows, slab_cols], slab(sp), sk.at[0], rk.at[0], sp, mate)

    to_mate = lambda c: remote(db.at[0, c], db.at[1, c], s1.at[c], r1.at[c], sp, mate)
    to_peer = lambda c: remote(db.at[0, c], db.at[2, c], s2.at[c], r2.at[c], sp, peer)
    pass_on = lambda c: remote(db.at[1, c], db.at[3, c], s3.at[c], r3.at[c], sp, peer)
    partial = lambda c: remote(pb.at[c], pb.at[c], s4.at[c], r4.at[c], sp, mate)
    to_right = remote(db.at[0, chunks - 1], hl.at[0], sh.at[0], rh.at[0], right, z)
    to_left = remote(db.at[0, 0], hl.at[1], sh.at[1], rh.at[1], left, z)

    def plan(out_slab, in_slab, at, target):
        return (remote(slab(out_slab), slab(out_slab), sk.at[at], rk.at[at], target, z),
                remote(slab(in_slab), slab(in_slab), sk.at[at], rk.at[at], target, z))

    over_x = plan(sp, by_x, 1, by_x)
    over_y = plan(sp, by_y, 2, by_y)
    over_xy = plan(by_x, by_xy, 3, by_y)
    over_core = [plan(mine, mine + by_core - sp, 4 + i, by_core)
                 for i, mine in enumerate((sp, by_x, by_y, by_xy))]

    @pl.when(jnp.logical_not(mid))
    def _():
        kern_out.start()

    load_d.wait()

    def cols(c):
        return pl.ds(pl.multiple_of(c * WIDE, WIDE), WIDE)

    def rows(r):
        return pl.ds(pl.multiple_of(r * TILE, TILE), TILE)

    def loop(n, body):
        def step(i, carry):
            body(i)
            return carry
        lax.fori_loop(0, n, step, 0)

    def span(lo, hi, body):
        def step(i, carry):
            body(i)
            return carry
        lax.fori_loop(lo, hi, step, 0)

    def lower(c):
        def tile(r):
            db[0, c, rows(r), :] = d32[rows(r), cols(c)].astype(jnp.bfloat16)
        loop(PARTS, tile)

    def lower_send(c):
        lower(c)

        @pl.when(mid)
        def _():
            to_peer(c).start()
            to_mate(c).start()

    loop(chunks, lower_send)
    to_right.start()
    to_left.start()

    @pl.when(jnp.logical_not(mid))
    def _():
        kern_out.wait_send()
        loop(chunks, lambda c: to_mate(c).start())

    load_k.wait()
    to_right.wait_recv()
    to_left.wait_recv()

    lane = lax.broadcasted_iota(jnp.int32, (TILE, WIDE), 1)
    low_wall = lax.rem(lane, NY) == 0
    up_wall = lax.rem(lane, NY) == NY - 1

    def dot(ref, r, block, slot, c):
        k_cols = pl.ds(pl.multiple_of(block * ROWS, ROWS), ROWS)
        return jnp.dot(ref[rows(r), k_cols], db[slot, c], preferred_element_type=jnp.float32)

    def local(c):
        prev_at = cols(jnp.maximum(c - 1, 0))
        next_at = cols(jnp.minimum(c + 1, chunks - 1))

        def tile(r):
            at = rows(r)
            g = d32[at, cols(c)]
            prev = jnp.where(c == 0, hl[0, at, :].astype(jnp.float32), d32[at, prev_at])
            after = jnp.where(c == chunks - 1, hl[1, at, :].astype(jnp.float32), d32[at, next_at])
            g_left = jnp.where(lane < NY, pltpu.roll(prev, NY, 1), pltpu.roll(g, NY, 1))
            g_right = jnp.where(lane >= WIDE - NY, pltpu.roll(after, WIDE - NY, 1),
                                pltpu.roll(g, WIDE - NY, 1))
            below = jnp.where(low_wall, 0.0, pltpu.roll(g, 1, 1))
            above = jnp.where(up_wall, 0.0, pltpu.roll(g, WIDE - 1, 1))
            moved = (coef[at, 0:1] * (g - g_left) + coef[at, 1:2] * (g_right - g)
                     + coef[at, 2:3] * (g - below) + coef[at, 3:4] * (above - g))
            out[at, cols(c)] = g - moved - coef[at, 4:5] * g + dot(ks, r, z, 0, c)
        loop(PARTS, tile)

    loop(chunks, local)

    def add_mate(c):
        def tile(r):
            out[rows(r), cols(c)] += dot(ks, r, mate, 1, c)
        loop(PARTS, tile)

    @pl.when(jnp.logical_not(mid))
    def _():
        def mates(c):
            to_mate(c).wait_recv()
            add_mate(c)
        loop(chunks, mates)

        def others(c):
            partial(c).wait_recv()

            def tile(r):
                out[rows(r), cols(c)] += pb[c, rows(r), :].astype(jnp.float32)
            loop(PARTS, tile)
        loop(chunks, others)
        loop(chunks, lambda c: to_mate(c).wait_send())

    @pl.when(mid)
    def _():
        def mates(c):
            to_mate(c).wait_recv()
            pass_on(c).start()
            add_mate(c)

        kern_out.wait_recv()
        over_x[0].start()
        over_y[0].start()
        span(0, 2, mates)
        over_x[1].wait_recv()
        over_xy[0].start()
        span(2, 5, mates)
        over_y[1].wait_recv()
        over_xy[1].wait_recv()
        for pair in over_core:
            pair[0].start()
        for pair in over_core:
            pair[1].wait_recv()

        base = (1 - half) * 2

        def finish(c):
            @pl.when(c + 5 < chunks)
            def _():
                mates(c + 5)

            to_peer(c).wait_recv()
            pass_on(c).wait_recv()

            def flux_tile(r, total):
                at = rows(r)
                part = (coef[at, 9:10] * db[2, c, at, :].astype(jnp.float32)
                        + coef[at, 10:11] * db[3, c, at, :].astype(jnp.float32))
                return total + jnp.sum(part, axis=0, keepdims=True)
            flux = lax.fori_loop(0, PARTS, flux_tile, jnp.zeros((1, WIDE), jnp.float32))
            diffuse = flux * lanes[0:1, cols(c)]
            specular = lanes[1:2, cols(c)]

            def send_tile(r):
                at, flipped = rows(r), rows(PARTS - 1 - r)
                wall = (coef[at, 7:8] * diffuse
                        + coef[at, 8:9] * specular * db[3, c, flipped, :].astype(jnp.float32))
                total = wall + dot(ke, r, peer - base, 2, c) + dot(ke, r, far - base, 3, c)
                pb[c, at, :] = total.astype(jnp.bfloat16)
            loop(PARTS, send_tile)
            partial(c).start()

            def own_tile(r):
                at, flipped = rows(r), rows(PARTS - 1 - r)
                wall = (coef[at, 5:6] * diffuse
                        + coef[at, 6:7] * specular * db[2, c, flipped, :].astype(jnp.float32))
                out[at, cols(c)] += wall + dot(ks, r, peer, 2, c) + dot(ks, r, far, 3, c)
            loop(PARTS, own_tile)

        loop(chunks, finish)
        for pair in (over_x, over_y, over_xy, *over_core):
            pair[0].wait_send()

        def drain(c):
            to_mate(c).wait_send()
            to_peer(c).wait_send()
            pass_on(c).wait_send()
            partial(c).wait_send()
        loop(chunks, drain)

    to_right.wait_send()
    to_left.wait_send()


def per_device_line(distribution, kernel, frequency, accommodation, wall_class):
    vel_rows, cell_count = distribution.shape
    chunks = cell_count // WIDE
    z = lax.axis_index("vel")
    mate = z + 1 - 2 * lax.rem(z, 2)
    row = lax.iota(jnp.int32, vel_rows)
    normal_sum, outflow = grid_constants()

    def parts(block):
        vx, vy, vz = velocity_parts(block * vel_rows + row)
        speed = jnp.abs(vy)
        return vx, vy, speed, jnp.exp(-0.5 * (vx * vx + vy * vy + vz * vz)) / normal_sum

    vx, vy, speed, maxwell = parts(z)
    _, _, mate_speed, mate_maxwell = parts(mate)
    _, _, peer_speed, _ = parts(3 - z)
    _, _, far_speed, _ = parts(3 - mate)
    values = [
        courant_x * jnp.maximum(vx, 0.0), courant_x * jnp.minimum(vx, 0.0),
        courant_y * jnp.maximum(vy, 0.0), courant_y * jnp.minimum(vy, 0.0), frequency,
        courant_y * speed * maxwell / outflow, courant_y * speed,
        courant_y * mate_speed * mate_maxwell / outflow, courant_y * mate_speed,
        peer_speed, far_speed,
    ]
    place = lax.broadcasted_iota(jnp.int32, (vel_rows, WIDE), 1)
    coef = jnp.zeros((vel_rows, WIDE), jnp.float32)
    for i, value in enumerate(values):
        coef = jnp.where(place == i, value[:, None], coef)
    low_side = z >= 2
    classes = jnp.where(low_side, wall_class[0], wall_class[1])
    ids = lax.iota(jnp.int32, NCLASS)
    alpha = jnp.sum(jnp.where(classes[:, None] == ids[None, :], accommodation[None, :], 0.0), axis=1)
    wall_y = jnp.where(low_side, 0, NY - 1)
    at_wall = lax.iota(jnp.int32, NY) == wall_y
    both = jnp.stack([alpha, 1.0 - alpha])
    lanes = jnp.where(at_wall[None, None, :], both[:, :, None], 0.0).reshape(2, cell_count)
    lanes = jnp.concatenate([lanes, jnp.zeros((6, cell_count), jnp.float32)])
    dma = pltpu.SemaphoreType.DMA
    vmem = pl.BlockSpec(memory_space=pltpu.VMEM)
    any_space = pl.BlockSpec(memory_space=pl.ANY)
    return pl.pallas_call(
        gain_kernel,
        out_shape=jax.ShapeDtypeStruct(distribution.shape, jnp.float32),
        in_specs=[any_space, any_space, vmem, vmem],
        out_specs=vmem,
        scratch_shapes=[
            pltpu.VMEM((ROWS, cell_count), jnp.float32),
            pltpu.VMEM((ROWS, PARTS * ROWS), jnp.bfloat16),
            pltpu.VMEM((ROWS, 2 * ROWS), jnp.bfloat16),
            pltpu.VMEM((PARTS, chunks, ROWS, WIDE), jnp.bfloat16),
            pltpu.VMEM((chunks, ROWS, WIDE), jnp.bfloat16),
            pltpu.VMEM((2, ROWS, WIDE), jnp.bfloat16),
            dma((2,)),
            *[dma((chunks,))] * 8,
            dma((8,)), dma((8,)), dma((2,)), dma((2,)),
        ],
        compiler_params=pltpu.CompilerParams(
            collective_id=0, has_side_effects=True, vmem_limit_bytes=56 << 20),
        cost_estimate=pl.CostEstimate(flops=12 * ROWS ** 3, bytes_accessed=24 << 20, transcendentals=0),
    )(distribution, kernel, coef, lanes)


def solution(mesh):
    line = mesh.shape["vel"] == PARTS and mesh.shape["space"] == SPACE
    body = per_device_line if line else per_device
    placed = (P("vel", "space"), P("vel", None), P("vel"), P(), P(None, "space"))
    return jax.shard_map(
        body, mesh=mesh, in_specs=placed, out_specs=P("vel", "space"), check_vma=False
    )
```

```python
import math

import jax
import jax.numpy as jnp
from jax import lax
from jax.experimental import pallas as pl
from jax.experimental.pallas import tpu as pltpu
from jax.sharding import PartitionSpec as P

NV1 = 16
NY = 32
NCLASS = 8


courant_x = 0.05
courant_y = 0.15


def swapped(value, axis, distance):
    return lax.ppermute(value, axis, [(i, i ^ 1 << distance) for i in range(lax.axis_size(axis))])


def extended(value, sides, width):
    for axis, dim in sides:
        devices, length = (lax.axis_size(axis), value.shape[dim])
        up = [(i, (i + 1) % devices) for i in range(devices)]
        down = [(j, i) for i, j in up]
        last = lax.slice_in_dim(value, length - width, length, axis=dim)
        initial = lax.slice_in_dim(value, 0, width, axis=dim)
        before = lax.ppermute(last, axis, up)
        after = lax.ppermute(initial, axis, down)
        value = jnp.concatenate([before, value, after], axis=dim)
    return value


def velocity_parts(vel_index):
    spacing = 9.6 / NV1
    middle = (NV1 - 1) / 2.0
    index_y = vel_index // (NV1 * NV1)
    index_x = vel_index // NV1 % NV1
    index_z = vel_index % NV1
    vel_x = (index_x.astype(jnp.float32) - middle) * spacing
    vel_y = (index_y.astype(jnp.float32) - middle) * spacing
    vel_z = (index_z.astype(jnp.float32) - middle) * spacing
    return (vel_x, vel_y, vel_z)


def grid_constants():
    spacing = 9.6 / NV1
    middle = (NV1 - 1) / 2.0
    points = (lax.iota(jnp.int32, NV1).astype(jnp.float32) - middle) * spacing
    weights = jnp.exp(-0.5 * points * points)
    zsum = jnp.sum(weights)
    outflow = jnp.sum(jnp.where(points > 0, points * weights, 0.0)) / zsum
    return (zsum * zsum * zsum, outflow)


def per_device(distribution, kernel, frequency, accommodation, wall_class):
    vel_rows, cell_count = distribution.shape
    columns = cell_count // NY
    plane = NV1 * NV1
    rank = lax.axis_index("vel")
    vel_index = rank * vel_rows + lax.iota(jnp.int32, vel_rows)
    vel_x, vel_y, vel_z = velocity_parts(vel_index)
    normal_sum, outflow = grid_constants()
    maxwell = jnp.exp(-0.5 * (vel_x * vel_x + vel_y * vel_y + vel_z * vel_z)) / normal_sum
    lowered = distribution.astype(jnp.bfloat16)
    walls = jnp.stack([lowered[:, 0::NY], lowered[:, NY - 1 :: NY]])
    wide = walls.astype(jnp.float32)
    down_weight = jnp.where(vel_y < 0, -vel_y, 0.0)
    up_weight = jnp.where(vel_y > 0, vel_y, 0.0)
    partial_flux = jnp.stack(
        [
            jnp.sum(down_weight[:, None] * wide[0], axis=0),
            jnp.sum(up_weight[:, None] * wide[1], axis=0),
        ]
    )
    flux = lax.psum(partial_flux, "vel")
    mirrored = walls
    log_rows = vel_rows.bit_length() - 1
    log_devices = lax.axis_size("vel").bit_length() - 1
    log_plane = 2 * (NV1.bit_length() - 1)
    for bit_index in range(max(log_plane - log_rows, 0), log_devices):
        mirrored = swapped(mirrored, "vel", bit_index)
    if vel_rows > plane:
        mirrored = mirrored.reshape(2, vel_rows // plane, plane, columns)[:, ::-1].reshape(
            2, vel_rows, columns
        )
    mirrored = mirrored.astype(jnp.float32)
    sigma = flux / outflow
    class_ids = lax.iota(jnp.int32, NCLASS)
    alpha = jnp.sum(
        jnp.where(
            wall_class[:, :, None] == class_ids[None, None, :], accommodation[None, None, :], 0.0
        ),
        axis=2,
    )
    inflow = (
        alpha[:, None, :] * sigma[:, None, :] * maxwell[None, :, None]
        + (1.0 - alpha)[:, None, :] * mirrored
    )
    padded = extended(distribution.astype(jnp.bfloat16), (("space", 1),), NY).astype(
        distribution.dtype
    )
    left = padded[:, :cell_count]
    right = padded[:, 2 * NY :]
    y_place = lax.iota(jnp.int32, cell_count) % NY
    below = jnp.concatenate([distribution[:, :1], distribution[:, :-1]], axis=1)
    below = jnp.where(y_place[None, :] == 0, jnp.repeat(inflow[0], NY, axis=1), below)
    above = jnp.concatenate([distribution[:, 1:], distribution[:, -1:]], axis=1)
    above = jnp.where(y_place[None, :] == NY - 1, jnp.repeat(inflow[1], NY, axis=1), above)
    move_x = courant_x * (
        jnp.maximum(vel_x, 0.0)[:, None] * (distribution - left)
        + jnp.minimum(vel_x, 0.0)[:, None] * (right - distribution)
    )
    move_y = courant_y * (
        jnp.maximum(vel_y, 0.0)[:, None] * (distribution - below)
        + jnp.minimum(vel_y, 0.0)[:, None] * (above - distribution)
    )
    moved = move_x + move_y
    shard_piece = lax.all_gather(lowered, "vel", axis=0, tiled=True)
    running = jnp.dot(kernel, shard_piece, preferred_element_type=jnp.float32)
    piece_walls = jnp.stack([shard_piece[:, 0::NY], shard_piece[:, NY - 1 :: NY]])
    wall_store = piece_walls
    gain, wall_store = (running, wall_store)
    return distribution - moved - frequency[:, None] * distribution + gain


WIDE = 128
ROWS = 1024
TILE = NV1 * NV1
PARTS = 4
SPACE = 8


def step_kernel(dist, kern, freq, accom, wall_class, out, d32, ks, ke, db, pb, hl, coef, fcol, acc,
                lsem, s1, r1, s2, r2, s3, r3, s4, r4, sk, rk, sh, rh):
    chunks = dist.shape[1] // WIDE
    per_chunk = WIDE // NY
    spacing, middle = 9.6 / NV1, (NV1 - 1) / 2.0
    points = [(i - middle) * spacing for i in range(NV1)]
    zsum = sum(math.exp(-0.5 * p * p) for p in points)
    outflow = sum(p * math.exp(-0.5 * p * p) for p in points if p > 0) / zsum
    sp, z = lax.axis_index("space"), lax.axis_index("vel")
    half = lax.div(z, 2)
    mid = lax.rem(z, 2) + half == 1
    mate = z + 1 - 2 * lax.rem(z, 2)
    peer = 3 - z
    far = 3 - mate
    by_core = sp + 1 - 2 * lax.rem(sp, 2)
    by_x = sp + 2 - 4 * lax.rem(lax.div(sp, 2), 2)
    by_y = sp + 4 - 8 * lax.div(sp, 4)
    by_xy = by_x + by_y - sp
    right = lax.rem(sp + 1, SPACE)
    left = lax.rem(sp + SPACE - 1, SPACE)

    def remote(src, dst, send, recv, space, vel):
        return pltpu.make_async_remote_copy(
            src_ref=src, dst_ref=dst, send_sem=send, recv_sem=recv,
            device_id={"space": space, "vel": vel}, device_id_type=pl.DeviceIdType.MESH)

    load_d = pltpu.make_async_copy(dist, d32, lsem.at[0])
    load_k = pltpu.make_async_copy(kern, ks, lsem.at[1])
    load_d.start()
    load_k.start()

    barrier = pltpu.get_barrier_semaphore()

    def greet(space, vel):
        pl.semaphore_signal(barrier, inc=1, device_id={"space": space, "vel": vel},
                            device_id_type=pl.DeviceIdType.MESH)

    greet(sp, mate)
    greet(left, z)
    greet(right, z)

    @pl.when(mid)
    def _():
        greet(sp, peer)
        greet(by_core, z)
        greet(by_x, z)
        greet(by_y, z)

    def slab(owner):
        return ke.at[pl.ds(pl.multiple_of(owner * (ROWS // SPACE), ROWS // SPACE), ROWS // SPACE)]

    slab_rows = pl.ds(pl.multiple_of(sp * (ROWS // SPACE), ROWS // SPACE), ROWS // SPACE)
    slab_cols = pl.ds(pl.multiple_of((1 - half) * 2 * ROWS, 2 * ROWS), 2 * ROWS)
    kern_out = remote(kern.at[slab_rows, slab_cols], slab(sp), sk.at[0], rk.at[0], sp, mate)

    to_mate = lambda c: remote(db.at[0, c], db.at[1, c], s1.at[c], r1.at[c], sp, mate)
    to_peer = lambda c: remote(db.at[0, c], db.at[2, c], s2.at[c], r2.at[c], sp, peer)
    pass_on = lambda c: remote(db.at[1, c], db.at[3, c], s3.at[c], r3.at[c], sp, peer)
    def partial(c, r):
        part = pb.at[c, pl.ds(pl.multiple_of(r * TILE, TILE), TILE)]
        return remote(part, part, s4.at[c, r], r4.at[c, r], sp, mate)

    to_right = remote(db.at[0, chunks - 1], hl.at[0], sh.at[0], rh.at[0], right, z)
    to_left = remote(db.at[0, 0], hl.at[1], sh.at[1], rh.at[1], left, z)

    def plan(out_slab, in_slab, at, target):
        return (remote(slab(out_slab), slab(out_slab), sk.at[at], rk.at[at], target, z),
                remote(slab(in_slab), slab(in_slab), sk.at[at], rk.at[at], target, z))

    over_x = plan(sp, by_x, 1, by_x)
    over_y = plan(sp, by_y, 2, by_y)
    over_xy = plan(by_x, by_xy, 3, by_y)
    over_core = [plan(mine, mine + by_core - sp, 4 + i, by_core)
                 for i, mine in enumerate((sp, by_x, by_y, by_xy))]

    load_d.wait()

    def cols(c):
        return pl.ds(pl.multiple_of(c * WIDE, WIDE), WIDE)

    def rows(r):
        return pl.ds(pl.multiple_of(r * TILE, TILE), TILE)

    def loop(n, body):
        def step(i, carry):
            body(i)
            return carry
        lax.fori_loop(0, n, step, 0)

    def span(lo, hi, body):
        def step(i, carry):
            body(i)
            return carry
        lax.fori_loop(lo, hi, step, 0)

    def lower(c):
        def tile(r):
            db[0, c, rows(r), :] = d32[rows(r), cols(c)].astype(jnp.bfloat16)
        loop(PARTS, tile)

    loop(chunks, lower)

    @pl.when(mid)
    def _():
        pl.semaphore_wait(barrier, 7)

        def send(c):
            to_peer(c).start()
            to_mate(c).start()
        loop(chunks, send)

    @pl.when(jnp.logical_not(mid))
    def _():
        pl.semaphore_wait(barrier, 3)
        kern_out.start()

    to_right.start()
    to_left.start()

    plane = lax.broadcasted_iota(jnp.int32, (TILE, WIDE), 0)
    place = lax.broadcasted_iota(jnp.int32, (TILE, WIDE), 1)
    vel_x = (lax.div(plane, NV1).astype(jnp.float32) - middle) * spacing
    vel_z = (lax.rem(plane, NV1).astype(jnp.float32) - middle) * spacing
    coef[...] = jnp.where(
        place == 0, courant_x * jnp.maximum(vel_x, 0.0),
        jnp.where(place == 1, courant_x * jnp.minimum(vel_x, 0.0), vel_x * vel_x + vel_z * vel_z))
    square = (lax.broadcasted_iota(jnp.int32, (WIDE, WIDE), 0)
              == lax.broadcasted_iota(jnp.int32, (WIDE, WIDE), 1))
    for i in range(ROWS // WIDE):
        fcol[i * WIDE : (i + 1) * WIDE, 0:1] = jnp.sum(
            jnp.where(square, freq[i : i + 1, :], 0.0), axis=1, keepdims=True)

    def vel_y(block, r):
        return ((block * PARTS + r).astype(jnp.float32) - middle) * spacing

    def speed(block, r):
        return jnp.maximum(vel_y(block, r), -vel_y(block, r))

    def maxwell(block, r):
        vy = vel_y(block, r)
        return jnp.exp(-0.5 * (coef[:, 2:3] + vy * vy)) * (1.0 / zsum ** 3)

    @pl.when(jnp.logical_not(mid))
    def _():
        kern_out.wait_send()
        loop(chunks, lambda c: to_mate(c).start())

    load_k.wait()
    to_right.wait_recv()
    to_left.wait_recv()

    lane = lax.broadcasted_iota(jnp.int32, (TILE, WIDE), 1)
    low_wall = lax.rem(lane, NY) == 0
    up_wall = lax.rem(lane, NY) == NY - 1

    def dot(ref, r, block, slot, c):
        k_cols = pl.ds(pl.multiple_of(block * ROWS, ROWS), ROWS)
        return jnp.dot(ref[rows(r), k_cols], db[slot, c], preferred_element_type=jnp.float32)

    def local(c):
        prev_at = cols(jnp.maximum(c - 1, 0))
        next_at = cols(jnp.minimum(c + 1, chunks - 1))

        def tile(r):
            at = rows(r)
            vy = vel_y(z, r)
            g = d32[at, cols(c)]
            prev = jnp.where(c == 0, hl[0, at, :].astype(jnp.float32), d32[at, prev_at])
            after = jnp.where(c == chunks - 1, hl[1, at, :].astype(jnp.float32), d32[at, next_at])
            g_left = jnp.where(lane < NY, pltpu.roll(prev, NY, 1), pltpu.roll(g, NY, 1))
            g_right = jnp.where(lane >= WIDE - NY, pltpu.roll(after, WIDE - NY, 1),
                                pltpu.roll(g, WIDE - NY, 1))
            below = jnp.where(low_wall, 0.0, pltpu.roll(g, 1, 1))
            above = jnp.where(up_wall, 0.0, pltpu.roll(g, WIDE - 1, 1))
            moved = (coef[:, 0:1] * (g - g_left) + coef[:, 1:2] * (g_right - g)
                     + courant_y * jnp.maximum(vy, 0.0) * (g - below)
                     + courant_y * jnp.minimum(vy, 0.0) * (above - g))
            out[at, cols(c)] = g - moved - fcol[at, 0:1] * g + dot(ks, r, z, 0, c)
        loop(PARTS, tile)

    loop(chunks, local)

    def add_mate(c):
        def tile(r):
            out[rows(r), cols(c)] += dot(ks, r, mate, 1, c)
        loop(PARTS, tile)

    @pl.when(jnp.logical_not(mid))
    def _():
        def mates(c):
            to_mate(c).wait_recv()
            add_mate(c)
        loop(chunks, mates)

        def others(c):
            def tile(r):
                partial(c, r).wait_recv()
                out[rows(r), cols(c)] += pb[c, rows(r), :].astype(jnp.float32)
            loop(PARTS, tile)
        loop(chunks, others)
        loop(chunks, lambda c: to_mate(c).wait_send())

    @pl.when(mid)
    def _():
        def mates(c):
            to_mate(c).wait_recv()
            pass_on(c).start()
            add_mate(c)

        kern_out.wait_recv()
        over_x[0].start()
        over_y[0].start()
        span(0, 2, mates)
        over_x[1].wait_recv()
        over_xy[0].start()
        span(2, 5, mates)
        over_y[1].wait_recv()
        over_xy[1].wait_recv()
        for pair in over_core:
            pair[0].start()
        for pair in over_core:
            pair[1].wait_recv()

        base = (1 - half) * 2

        def finish(c):
            @pl.when(c + 5 < chunks)
            def _():
                mates(c + 5)

            to_peer(c).wait_recv()

            def near_tile(r, total):
                at = rows(r)
                acc[at, :] = dot(ke, r, peer - base, 2, c)
                out[at, cols(c)] += dot(ks, r, peer, 2, c)
                part = speed(peer, r) * db[2, c, at, :].astype(jnp.float32)
                return total + jnp.sum(part, axis=0, keepdims=True)
            flux = lax.fori_loop(0, PARTS, near_tile, jnp.zeros((1, WIDE), jnp.float32))

            pass_on(c).wait_recv()

            def flux_tile(r, total):
                part = speed(far, r) * db[3, c, rows(r), :].astype(jnp.float32)
                return total + jnp.sum(part, axis=0, keepdims=True)
            flux = lax.fori_loop(0, PARTS, flux_tile, flux)

            spot = lax.broadcasted_iota(jnp.int32, (1, WIDE), 1)
            alpha = jnp.zeros((1, WIDE), jnp.float32)
            specular = alpha
            for j in range(per_chunk):
                value = accom[wall_class[1 - half, c * per_chunk + j]]
                here = spot == j * NY + (1 - half) * (NY - 1)
                alpha = jnp.where(here, value, alpha)
                specular = jnp.where(here, 1.0 - value, specular)
            diffuse = flux * alpha * (1.0 / outflow)

            def wall(block, r, slot):
                mirror = db[slot, c, rows(PARTS - 1 - r), :].astype(jnp.float32)
                return courant_y * speed(block, r) * (diffuse * maxwell(block, r) + specular * mirror)

            def send_tile(r):
                at = rows(r)
                total = acc[at, :] + wall(mate, r, 3) + dot(ke, r, far - base, 3, c)
                pb[c, at, :] = total.astype(jnp.bfloat16)
                partial(c, r).start()
            loop(PARTS, send_tile)

            def own_tile(r):
                at = rows(r)
                out[at, cols(c)] += wall(z, r, 2) + dot(ks, r, far, 3, c)
            loop(PARTS, own_tile)

        loop(chunks, finish)
        for pair in (over_x, over_y, over_xy, *over_core):
            pair[0].wait_send()

        def drain(c):
            to_mate(c).wait_send()
            to_peer(c).wait_send()
            pass_on(c).wait_send()
            loop(PARTS, lambda r: partial(c, r).wait_send())
        loop(chunks, drain)

    to_right.wait_send()
    to_left.wait_send()


def per_device_line(distribution, kernel, frequency, accommodation, wall_class):
    cell_count = distribution.shape[1]
    chunks = cell_count // WIDE
    dma = pltpu.SemaphoreType.DMA
    vmem = pl.BlockSpec(memory_space=pltpu.VMEM)
    smem = pl.BlockSpec(memory_space=pltpu.SMEM)
    any_space = pl.BlockSpec(memory_space=pl.ANY)
    return pl.pallas_call(
        step_kernel,
        out_shape=pltpu.VMEM(distribution.shape, jnp.float32),
        in_specs=[any_space, any_space, vmem, smem, smem],
        out_specs=vmem,
        scratch_shapes=[
            pltpu.VMEM((ROWS, cell_count), jnp.float32),
            pltpu.VMEM((ROWS, PARTS * ROWS), jnp.bfloat16),
            pltpu.VMEM((ROWS, 2 * ROWS), jnp.bfloat16),
            pltpu.VMEM((PARTS, chunks, ROWS, WIDE), jnp.bfloat16),
            pltpu.VMEM((chunks, ROWS, WIDE), jnp.bfloat16),
            pltpu.VMEM((2, ROWS, WIDE), jnp.bfloat16),
            pltpu.VMEM((TILE, WIDE), jnp.float32),
            pltpu.VMEM((ROWS, WIDE), jnp.float32),
            pltpu.VMEM((ROWS, WIDE), jnp.float32),
            dma((2,)),
            *[dma((chunks,))] * 6, dma((chunks, PARTS)), dma((chunks, PARTS)),
            dma((8,)), dma((8,)), dma((2,)), dma((2,)),
        ],
        compiler_params=pltpu.CompilerParams(
            collective_id=0, has_side_effects=True, vmem_limit_bytes=56 << 20),
        cost_estimate=pl.CostEstimate(flops=12 * ROWS ** 3, bytes_accessed=24 << 20, transcendentals=0),
    )(distribution, kernel, frequency.reshape(ROWS // WIDE, WIDE), accommodation, wall_class)


def solution(mesh):
    line = mesh.shape["vel"] == PARTS and mesh.shape["space"] == SPACE
    body = per_device_line if line else per_device
    placed = (P("vel", "space"), P("vel", None), P("vel"), P(), P(None, "space"))
    return jax.shard_map(
        body, mesh=mesh, in_specs=placed, out_specs=P("vel", "space"), check_vma=False
    )
```

```python
import math

import jax
import jax.numpy as jnp
from jax import lax
from jax.experimental import pallas as pl
from jax.experimental.pallas import tpu as pltpu
from jax.sharding import PartitionSpec as P

NV1 = 16
NY = 32
NCLASS = 8


courant_x = 0.05
courant_y = 0.15


def swapped(value, axis, distance):
    return lax.ppermute(value, axis, [(i, i ^ 1 << distance) for i in range(lax.axis_size(axis))])


def extended(value, sides, width):
    for axis, dim in sides:
        devices, length = (lax.axis_size(axis), value.shape[dim])
        up = [(i, (i + 1) % devices) for i in range(devices)]
        down = [(j, i) for i, j in up]
        last = lax.slice_in_dim(value, length - width, length, axis=dim)
        initial = lax.slice_in_dim(value, 0, width, axis=dim)
        before = lax.ppermute(last, axis, up)
        after = lax.ppermute(initial, axis, down)
        value = jnp.concatenate([before, value, after], axis=dim)
    return value


def velocity_parts(vel_index):
    spacing = 9.6 / NV1
    middle = (NV1 - 1) / 2.0
    index_y = vel_index // (NV1 * NV1)
    index_x = vel_index // NV1 % NV1
    index_z = vel_index % NV1
    vel_x = (index_x.astype(jnp.float32) - middle) * spacing
    vel_y = (index_y.astype(jnp.float32) - middle) * spacing
    vel_z = (index_z.astype(jnp.float32) - middle) * spacing
    return (vel_x, vel_y, vel_z)


def grid_constants():
    spacing = 9.6 / NV1
    middle = (NV1 - 1) / 2.0
    points = (lax.iota(jnp.int32, NV1).astype(jnp.float32) - middle) * spacing
    weights = jnp.exp(-0.5 * points * points)
    zsum = jnp.sum(weights)
    outflow = jnp.sum(jnp.where(points > 0, points * weights, 0.0)) / zsum
    return (zsum * zsum * zsum, outflow)


def per_device(distribution, kernel, frequency, accommodation, wall_class):
    vel_rows, cell_count = distribution.shape
    columns = cell_count // NY
    plane = NV1 * NV1
    rank = lax.axis_index("vel")
    vel_index = rank * vel_rows + lax.iota(jnp.int32, vel_rows)
    vel_x, vel_y, vel_z = velocity_parts(vel_index)
    normal_sum, outflow = grid_constants()
    maxwell = jnp.exp(-0.5 * (vel_x * vel_x + vel_y * vel_y + vel_z * vel_z)) / normal_sum
    lowered = distribution.astype(jnp.bfloat16)
    walls = jnp.stack([lowered[:, 0::NY], lowered[:, NY - 1 :: NY]])
    wide = walls.astype(jnp.float32)
    down_weight = jnp.where(vel_y < 0, -vel_y, 0.0)
    up_weight = jnp.where(vel_y > 0, vel_y, 0.0)
    partial_flux = jnp.stack(
        [
            jnp.sum(down_weight[:, None] * wide[0], axis=0),
            jnp.sum(up_weight[:, None] * wide[1], axis=0),
        ]
    )
    flux = lax.psum(partial_flux, "vel")
    mirrored = walls
    log_rows = vel_rows.bit_length() - 1
    log_devices = lax.axis_size("vel").bit_length() - 1
    log_plane = 2 * (NV1.bit_length() - 1)
    for bit_index in range(max(log_plane - log_rows, 0), log_devices):
        mirrored = swapped(mirrored, "vel", bit_index)
    if vel_rows > plane:
        mirrored = mirrored.reshape(2, vel_rows // plane, plane, columns)[:, ::-1].reshape(
            2, vel_rows, columns
        )
    mirrored = mirrored.astype(jnp.float32)
    sigma = flux / outflow
    class_ids = lax.iota(jnp.int32, NCLASS)
    alpha = jnp.sum(
        jnp.where(
            wall_class[:, :, None] == class_ids[None, None, :], accommodation[None, None, :], 0.0
        ),
        axis=2,
    )
    inflow = (
        alpha[:, None, :] * sigma[:, None, :] * maxwell[None, :, None]
        + (1.0 - alpha)[:, None, :] * mirrored
    )
    padded = extended(distribution.astype(jnp.bfloat16), (("space", 1),), NY).astype(
        distribution.dtype
    )
    left = padded[:, :cell_count]
    right = padded[:, 2 * NY :]
    y_place = lax.iota(jnp.int32, cell_count) % NY
    below = jnp.concatenate([distribution[:, :1], distribution[:, :-1]], axis=1)
    below = jnp.where(y_place[None, :] == 0, jnp.repeat(inflow[0], NY, axis=1), below)
    above = jnp.concatenate([distribution[:, 1:], distribution[:, -1:]], axis=1)
    above = jnp.where(y_place[None, :] == NY - 1, jnp.repeat(inflow[1], NY, axis=1), above)
    move_x = courant_x * (
        jnp.maximum(vel_x, 0.0)[:, None] * (distribution - left)
        + jnp.minimum(vel_x, 0.0)[:, None] * (right - distribution)
    )
    move_y = courant_y * (
        jnp.maximum(vel_y, 0.0)[:, None] * (distribution - below)
        + jnp.minimum(vel_y, 0.0)[:, None] * (above - distribution)
    )
    moved = move_x + move_y
    shard_piece = lax.all_gather(lowered, "vel", axis=0, tiled=True)
    running = jnp.dot(kernel, shard_piece, preferred_element_type=jnp.float32)
    piece_walls = jnp.stack([shard_piece[:, 0::NY], shard_piece[:, NY - 1 :: NY]])
    wall_store = piece_walls
    gain, wall_store = (running, wall_store)
    return distribution - moved - frequency[:, None] * distribution + gain


WIDE = 128
ROWS = 1024
TILE = NV1 * NV1
PARTS = 4
SPACE = 8


def step_kernel(dist, kern, freq, accom, wall_class, out, d32, ks, ke, db, pb, hl, coef, fcol, acc,
                lsem, s1, r1, s2, r2, s3, r3, s4, r4, s5, r5, s6, r6, sk, rk, sh, rh):
    chunks = dist.shape[1] // WIDE
    per_chunk = WIDE // NY
    spacing, middle = 9.6 / NV1, (NV1 - 1) / 2.0
    points = [(i - middle) * spacing for i in range(NV1)]
    zsum = sum(math.exp(-0.5 * p * p) for p in points)
    outflow = sum(p * math.exp(-0.5 * p * p) for p in points if p > 0) / zsum
    sp, z = lax.axis_index("space"), lax.axis_index("vel")
    half = lax.div(z, 2)
    mid = lax.rem(z, 2) + half == 1
    mate = z + 1 - 2 * lax.rem(z, 2)
    peer = 3 - z
    far = 3 - mate
    by_core = sp + 1 - 2 * lax.rem(sp, 2)
    by_x = sp + 2 - 4 * lax.rem(lax.div(sp, 2), 2)
    by_y = sp + 4 - 8 * lax.div(sp, 4)
    by_xy = by_x + by_y - sp
    right = lax.rem(sp + 1, SPACE)
    left = lax.rem(sp + SPACE - 1, SPACE)

    def remote(src, dst, send, recv, space, vel):
        return pltpu.make_async_remote_copy(
            src_ref=src, dst_ref=dst, send_sem=send, recv_sem=recv,
            device_id={"space": space, "vel": vel}, device_id_type=pl.DeviceIdType.MESH)

    load_d = pltpu.make_async_copy(dist, d32, lsem.at[0])
    load_k = pltpu.make_async_copy(kern, ks, lsem.at[1])
    load_d.start()
    load_k.start()

    barrier = pltpu.get_barrier_semaphore()

    def greet(space, vel):
        pl.semaphore_signal(barrier, inc=1, device_id={"space": space, "vel": vel},
                            device_id_type=pl.DeviceIdType.MESH)

    greet(sp, mate)
    greet(left, z)
    greet(right, z)

    @pl.when(mid)
    def _():
        greet(sp, peer)
        greet(by_core, z)
        greet(by_x, z)
        greet(by_y, z)

    def slab(owner):
        return ke.at[pl.ds(pl.multiple_of(owner * (ROWS // SPACE), ROWS // SPACE), ROWS // SPACE)]

    slab_rows = pl.ds(pl.multiple_of(sp * (ROWS // SPACE), ROWS // SPACE), ROWS // SPACE)
    slab_cols = pl.ds(pl.multiple_of((1 - half) * 2 * ROWS, 2 * ROWS), 2 * ROWS)
    kern_out = remote(kern.at[slab_rows, slab_cols], slab(sp), sk.at[0], rk.at[0], sp, mate)

    to_mate = lambda c: remote(db.at[0, c], db.at[1, c], s1.at[c], r1.at[c], sp, mate)
    to_peer = lambda c: remote(db.at[0, c], db.at[2, c], s2.at[c], r2.at[c], sp, peer)
    pass_on = lambda c: remote(db.at[1, c], db.at[3, c], s3.at[c], r3.at[c], sp, peer)
    last = chunks - 1

    def tail(slot, r, dst_slot, send, recv, vel):
        part = pl.ds(pl.multiple_of(r * TILE, TILE), TILE)
        return remote(db.at[slot, last, part], db.at[dst_slot, last, part],
                      send.at[r], recv.at[r], sp, vel)

    pass_last = lambda r: tail(1, r, 3, s5, r5, peer)
    raw_far = lambda r: tail(3, r, 3, s6, r6, mate)
    raw_near = remote(db.at[2, last], db.at[2, last], s6.at[PARTS], r6.at[PARTS], sp, mate)

    def partial(c, r):
        part = pb.at[c, pl.ds(pl.multiple_of(r * TILE, TILE), TILE)]
        return remote(part, part, s4.at[c, r], r4.at[c, r], sp, mate)

    to_right = remote(db.at[0, chunks - 1], hl.at[0], sh.at[0], rh.at[0], right, z)
    to_left = remote(db.at[0, 0], hl.at[1], sh.at[1], rh.at[1], left, z)

    def piece(owner, side):
        part = ROWS // SPACE // 2
        return ke.at[pl.ds(pl.multiple_of(owner * 2 * part + side * part, part), part)]

    def plan(sent, received, at, target):
        return (remote(sent, sent, sk.at[at], rk.at[at], target, z),
                remote(received, received, sk.at[at], rk.at[at], target, z))

    over_x = plan(slab(sp), slab(by_x), 1, by_x)
    over_y = plan(slab(sp), slab(by_y), 2, by_y)
    on_y = plan(piece(by_x, 0), piece(by_xy, 0), 3, by_y)
    on_x = plan(piece(by_y, 1), piece(by_xy, 1), 8, by_x)
    over_core = [plan(slab(mine), slab(mine + by_core - sp), 4 + i, by_core)
                 for i, mine in enumerate((sp, by_x, by_y, by_xy))]

    load_d.wait()

    def cols(c):
        return pl.ds(pl.multiple_of(c * WIDE, WIDE), WIDE)

    def rows(r):
        return pl.ds(pl.multiple_of(r * TILE, TILE), TILE)

    def loop(n, body):
        def step(i, carry):
            body(i)
            return carry
        lax.fori_loop(0, n, step, 0)

    def span(lo, hi, body):
        def step(i, carry):
            body(i)
            return carry
        lax.fori_loop(lo, hi, step, 0)

    def lower(c):
        def tile(r):
            db[0, c, rows(r), :] = d32[rows(r), cols(c)].astype(jnp.bfloat16)
        loop(PARTS, tile)

    loop(chunks, lower)

    @pl.when(mid)
    def _():
        pl.semaphore_wait(barrier, 7)

        def send(c):
            to_peer(c).start()
            to_mate(c).start()
        loop(chunks, send)

    @pl.when(jnp.logical_not(mid))
    def _():
        pl.semaphore_wait(barrier, 3)
        kern_out.start()

    to_right.start()
    to_left.start()

    plane = lax.broadcasted_iota(jnp.int32, (TILE, WIDE), 0)
    place = lax.broadcasted_iota(jnp.int32, (TILE, WIDE), 1)
    vel_x = (lax.div(plane, NV1).astype(jnp.float32) - middle) * spacing
    vel_z = (lax.rem(plane, NV1).astype(jnp.float32) - middle) * spacing
    coef[...] = jnp.where(
        place == 0, courant_x * jnp.maximum(vel_x, 0.0),
        jnp.where(place == 1, courant_x * jnp.minimum(vel_x, 0.0), vel_x * vel_x + vel_z * vel_z))
    square = (lax.broadcasted_iota(jnp.int32, (WIDE, WIDE), 0)
              == lax.broadcasted_iota(jnp.int32, (WIDE, WIDE), 1))
    for i in range(ROWS // WIDE):
        fcol[i * WIDE : (i + 1) * WIDE, 0:1] = jnp.sum(
            jnp.where(square, freq[i : i + 1, :], 0.0), axis=1, keepdims=True)

    def vel_y(block, r):
        return ((block * PARTS + r).astype(jnp.float32) - middle) * spacing

    def speed(block, r):
        return jnp.maximum(vel_y(block, r), -vel_y(block, r))

    def maxwell(block, r):
        vy = vel_y(block, r)
        return jnp.exp(-0.5 * (coef[:, 2:3] + vy * vy)) * (1.0 / zsum ** 3)

    @pl.when(jnp.logical_not(mid))
    def _():
        kern_out.wait_send()
        loop(chunks, lambda c: to_mate(c).start())

    load_k.wait()
    to_right.wait_recv()
    to_left.wait_recv()

    lane = lax.broadcasted_iota(jnp.int32, (TILE, WIDE), 1)
    low_wall = lax.rem(lane, NY) == 0
    up_wall = lax.rem(lane, NY) == NY - 1

    def dot(ref, r, block, slot, c):
        k_cols = pl.ds(pl.multiple_of(block * ROWS, ROWS), ROWS)
        return jnp.dot(ref[rows(r), k_cols], db[slot, c], preferred_element_type=jnp.float32)

    def local(c):
        prev_at = cols(jnp.maximum(c - 1, 0))
        next_at = cols(jnp.minimum(c + 1, chunks - 1))

        def tile(r):
            at = rows(r)
            vy = vel_y(z, r)
            g = d32[at, cols(c)]
            prev = jnp.where(c == 0, hl[0, at, :].astype(jnp.float32), d32[at, prev_at])
            after = jnp.where(c == chunks - 1, hl[1, at, :].astype(jnp.float32), d32[at, next_at])
            g_left = jnp.where(lane < NY, pltpu.roll(prev, NY, 1), pltpu.roll(g, NY, 1))
            g_right = jnp.where(lane >= WIDE - NY, pltpu.roll(after, WIDE - NY, 1),
                                pltpu.roll(g, WIDE - NY, 1))
            below = jnp.where(low_wall, 0.0, pltpu.roll(g, 1, 1))
            above = jnp.where(up_wall, 0.0, pltpu.roll(g, WIDE - 1, 1))
            moved = (coef[:, 0:1] * (g - g_left) + coef[:, 1:2] * (g_right - g)
                     + courant_y * jnp.maximum(vy, 0.0) * (g - below)
                     + courant_y * jnp.minimum(vy, 0.0) * (above - g))
            out[at, cols(c)] = g - moved - fcol[at, 0:1] * g + dot(ks, r, z, 0, c)
        loop(PARTS, tile)

    loop(chunks, local)

    def add_mate(c):
        def tile(r):
            out[rows(r), cols(c)] += dot(ks, r, mate, 1, c)
        loop(PARTS, tile)

    def flux_of(block, slot, c, start):
        def tile(r, total):
            part = speed(block, r) * db[slot, c, rows(r), :].astype(jnp.float32)
            return total + jnp.sum(part, axis=0, keepdims=True)
        return lax.fori_loop(0, PARTS, tile, start)

    def wall_rates(c, flux):
        spot = lax.broadcasted_iota(jnp.int32, (1, WIDE), 1)
        alpha = jnp.zeros((1, WIDE), jnp.float32)
        specular = alpha
        for j in range(per_chunk):
            value = accom[wall_class[1 - half, c * per_chunk + j]]
            here = spot == j * NY + (1 - half) * (NY - 1)
            alpha = jnp.where(here, value, alpha)
            specular = jnp.where(here, 1.0 - value, specular)
        return flux * alpha * (1.0 / outflow), specular

    def wall(rates, block, r, slot, c):
        diffuse, specular = rates
        mirror = db[slot, c, rows(PARTS - 1 - r), :].astype(jnp.float32)
        return courant_y * speed(block, r) * (diffuse * maxwell(block, r) + specular * mirror)

    near = jnp.where(mid, peer, far)
    rest = jnp.where(mid, far, peer)
    zero_flux = jnp.zeros((1, WIDE), jnp.float32)

    def close_near():
        def tile(r):
            out[rows(r), cols(last)] += dot(ks, r, near, 2, last)
        loop(PARTS, tile)
        return flux_of(near, 2, last, zero_flux)

    def close_rest(flux, mirror_slot):
        rates = wall_rates(last, flux_of(rest, 3, last, flux))

        def tile(r):
            out[rows(r), cols(last)] += (wall(rates, z, r, mirror_slot, last)
                                         + dot(ks, r, rest, 3, last))
        loop(PARTS, tile)

    @pl.when(jnp.logical_not(mid))
    def _():
        def mates(c):
            to_mate(c).wait_recv()
            add_mate(c)
        loop(chunks, mates)

        def others(c):
            def tile(r):
                partial(c, r).wait_recv()
                out[rows(r), cols(c)] += pb[c, rows(r), :].astype(jnp.float32)
            loop(PARTS, tile)
        loop(last, others)
        raw_near.wait_recv()
        flux = close_near()
        loop(PARTS, lambda r: raw_far(r).wait_recv())
        close_rest(flux, 3)
        loop(chunks, lambda c: to_mate(c).wait_send())

    @pl.when(mid)
    def _():
        def mates(c):
            to_mate(c).wait_recv()

            @pl.when(c < last)
            def _():
                pass_on(c).start()

            @pl.when(c == last)
            def _():
                loop(PARTS, lambda r: pass_last(r).start())

            add_mate(c)

        kern_out.wait_recv()
        over_x[0].start()
        over_y[0].start()
        span(0, 2, mates)
        over_x[1].wait_recv()
        on_y[0].start()
        over_y[1].wait_recv()
        on_x[0].start()
        span(2, 4, mates)
        on_y[1].wait_recv()
        on_x[1].wait_recv()
        for pair in over_core:
            pair[0].start()
        for pair in over_core:
            pair[1].wait_recv()

        base = (1 - half) * 2

        def finish(c):
            to_peer(c).wait_recv()

            def near_tile(r, total):
                at = rows(r)
                acc[at, :] = dot(ke, r, peer - base, 2, c)
                out[at, cols(c)] += dot(ks, r, peer, 2, c)
                part = speed(peer, r) * db[2, c, at, :].astype(jnp.float32)
                return total + jnp.sum(part, axis=0, keepdims=True)
            flux = lax.fori_loop(0, PARTS, near_tile, jnp.zeros((1, WIDE), jnp.float32))

            pass_on(c).wait_recv()

            rates = wall_rates(c, flux_of(far, 3, c, flux))

            def send_tile(r):
                at = rows(r)
                total = acc[at, :] + wall(rates, mate, r, 3, c) + dot(ke, r, far - base, 3, c)
                pb[c, at, :] = total.astype(jnp.bfloat16)
                partial(c, r).start()
            loop(PARTS, send_tile)

            @pl.when(c + 4 < chunks)
            def _():
                mates(c + 4)

            @pl.when(c == 3)
            def _():
                to_peer(last).wait_recv()
                raw_near.start()

            def own_tile(r):
                at = rows(r)
                out[at, cols(c)] += wall(rates, z, r, 2, c) + dot(ks, r, far, 3, c)
            loop(PARTS, own_tile)

        loop(last, finish)
        flux = close_near()

        def relay(r):
            pass_last(r).wait_recv()
            raw_far(r).start()
        loop(PARTS, relay)
        close_rest(flux, 2)
        for pair in (over_x, over_y, on_x, on_y, *over_core):
            pair[0].wait_send()

        def drain(c):
            to_mate(c).wait_send()
            to_peer(c).wait_send()

            @pl.when(c < last)
            def _():
                pass_on(c).wait_send()
                loop(PARTS, lambda r: partial(c, r).wait_send())
        loop(chunks, drain)
        raw_near.wait_send()

        def drain_last(r):
            pass_last(r).wait_send()
            raw_far(r).wait_send()
        loop(PARTS, drain_last)

    to_right.wait_send()
    to_left.wait_send()


def per_device_line(distribution, kernel, frequency, accommodation, wall_class):
    cell_count = distribution.shape[1]
    chunks = cell_count // WIDE
    dma = pltpu.SemaphoreType.DMA
    vmem = pl.BlockSpec(memory_space=pltpu.VMEM)
    smem = pl.BlockSpec(memory_space=pltpu.SMEM)
    any_space = pl.BlockSpec(memory_space=pl.ANY)
    return pl.pallas_call(
        step_kernel,
        out_shape=pltpu.VMEM(distribution.shape, jnp.float32),
        in_specs=[any_space, any_space, vmem, smem, smem],
        out_specs=vmem,
        scratch_shapes=[
            pltpu.VMEM((ROWS, cell_count), jnp.float32),
            pltpu.VMEM((ROWS, PARTS * ROWS), jnp.bfloat16),
            pltpu.VMEM((ROWS, 2 * ROWS), jnp.bfloat16),
            pltpu.VMEM((PARTS, chunks, ROWS, WIDE), jnp.bfloat16),
            pltpu.VMEM((chunks, ROWS, WIDE), jnp.bfloat16),
            pltpu.VMEM((2, ROWS, WIDE), jnp.bfloat16),
            pltpu.VMEM((TILE, WIDE), jnp.float32),
            pltpu.VMEM((ROWS, WIDE), jnp.float32),
            pltpu.VMEM((ROWS, WIDE), jnp.float32),
            dma((2,)),
            *[dma((chunks,))] * 6, dma((chunks, PARTS)), dma((chunks, PARTS)),
            dma((PARTS,)), dma((PARTS,)), dma((PARTS + 1,)), dma((PARTS + 1,)),
            dma((9,)), dma((9,)), dma((2,)), dma((2,)),
        ],
        compiler_params=pltpu.CompilerParams(
            collective_id=0, has_side_effects=True, vmem_limit_bytes=56 << 20),
        cost_estimate=pl.CostEstimate(flops=12 * ROWS ** 3, bytes_accessed=24 << 20, transcendentals=0),
    )(distribution, kernel, frequency.reshape(ROWS // WIDE, WIDE), accommodation, wall_class)


def solution(mesh):
    line = mesh.shape["vel"] == PARTS and mesh.shape["space"] == SPACE
    body = per_device_line if line else per_device
    placed = (P("vel", "space"), P("vel", None), P("vel"), P(), P(None, "space"))
    return jax.shard_map(
        body, mesh=mesh, in_specs=placed, out_specs=P("vel", "space"), check_vma=False
    )
```
